512 devices in a mesh: queue: 16 (over z_lo, core), heads: 32 (over x, z_hi, y).
Axes of the slice: x: 4, y: 4, z: 16 (z_hi: 2, z_lo: 8; z = z_hi * 8 + z_lo), core: 2. Of those that a mesh axis runs over, the one named last changes fastest.
Arguments:
- state: bfloat16 [65536, 4096], P(('queue', 'heads')), may hold values from -10 to 10
- fresh: bfloat16 [1, 4096, 4096], P(None, 'heads'), may hold values from -6 to 6
- frame_level: int32 [2, 256], P(None, 'queue'), may hold values from 0 to 47
- request: int32 [2, 16], P(None, 'queue'), may hold values from 0 to 3
- q_table: float32 [48, 4096], P(None, 'heads'), may hold values from -4.5 to 4.5
- k_table: float32 [48, 4096], P(None, 'heads'), may hold values from -4.5 to 4.5
- step_size: float32 [48], replicated, may hold values from 0.2 to 1
- reference_kv: bfloat16 [2, 4, 256, 4096], P(None, None, None, 'heads'), may hold values from -6 to 6
Outputs:
- final_state: bfloat16 [65536, 4096], P(('queue', 'heads'))
The draws below stay inside these ranges and needn't reach their ends.
All inputs are finite; a program needn't handle non-finite values.
Results may differ from the reference program's by a relative error of at most 0.0053.
Values may be sent and summed in bfloat16 or wider, within the bound.
A program may use at most 64 MiB of HBM per device.

```python
import math
import jax
import jax.numpy as jnp
from jax import lax

HDIM = 128
HEADS = 32
HD = 4096
FT = 256
FRAMES = 16
LEVELS = 48
REQS = 4
ITERS = 2
TOKENS = 65536
N_QUEUE = 16


def draw_state(key, part):
    key = jax.random.fold_in(key, 11)
    column = 0.6 * 3.0 ** (jnp.arange(HD, dtype=jnp.float32) / (HD - 1))
    drawn = jax.random.normal(key, (TOKENS, HD), jnp.float32) * column[None, :]
    return jnp.clip(drawn, -10.0, 10.0).astype(jnp.bfloat16)


def table_values(key):
    drawn = jnp.clip(jax.random.normal(key, (LEVELS, HD), jnp.float32), -4.5, 4.5)
    return drawn.astype(jnp.float32)


def draw_q_table(key, part):
    key = jax.random.fold_in(key, 23)
    return table_values(key)


def draw_k_table(key, part):
    key = jax.random.fold_in(key, 37)
    return table_values(key)


def plant(values, key, low, high):
    dims = values.shape
    spot = [jax.random.randint(jax.random.fold_in(key, axis), (), 0, dims[axis]) for axis in range(len(dims))]
    values = values.at[tuple(spot)].set(low)
    longest = dims.index(max(dims))
    spot[longest] = (spot[longest] + 1) % dims[longest]
    return values.at[tuple(spot)].set(high)


def block_levels(key, shape, shards, low, high):
    factor_of, own = 1.0, jax.random.fold_in(key, 6)
    for dim, blocks in shards:
        draws = jnp.exp(jax.random.uniform(jax.random.fold_in(own, dim), (blocks,), jnp.float32, low / len(shards), high / len(shards)))
        factor_of = factor_of * jnp.repeat(draws, shape[dim] // blocks).reshape([-1 if axis == dim else 1 for axis in range(len(shape))])
    return factor_of


def scatter_about(stream_key, dims, deviation, bound, cuts=(), held_as=jnp.bfloat16):
    gain = block_levels(stream_key, dims, cuts, -0.22, 0.18) if cuts else 1.0
    values = jax.random.normal(stream_key, dims, jnp.float32) * deviation * gain
    return jnp.minimum(jnp.maximum(values, -bound), bound).astype(held_as)


def setup_inputs(seed: int = 0) -> dict:
    arg_keys = jax.random.split(jax.random.key(seed), 9)
    state = draw_state(jax.random.fold_in(arg_keys[8], 71), 0)
    fresh = scatter_about(arg_keys[1], (ITERS - 1, FRAMES * FT, HD), 1.0, 6.0, ((1, 32),))
    frame_level = plant(jax.random.randint(arg_keys[2], (ITERS, N_QUEUE * FRAMES), 0, LEVELS), jax.random.fold_in(arg_keys[2], 1), 0, LEVELS - 1).astype(jnp.int32)
    request = plant(jax.random.randint(arg_keys[3], (ITERS, N_QUEUE), 0, REQS), jax.random.fold_in(arg_keys[3], 1), 0, REQS - 1).astype(jnp.int32)
    q_table = draw_q_table(jax.random.fold_in(arg_keys[8], 71), 0)
    k_table = draw_k_table(jax.random.fold_in(arg_keys[8], 71), 0)
    step_size = jnp.clip(jnp.exp(jax.random.uniform(arg_keys[6], (LEVELS,), jnp.float32, math.log(0.2), math.log(1.0))), 0.2, 1.0)
    reference_kv = scatter_about(arg_keys[7], (2, REQS, FT, HD), 1.0, 6.0, ((3, 32),))
    return {"state": state, "fresh": fresh, "frame_level": frame_level, "request": request, "q_table": q_table, "k_table": k_table, "step_size": step_size, "reference_kv": reference_kv}


epsilon = 1e-06
far_below = -1e+30

def frame_attention(queries, key_rows, values, has_prev, has_next, ref_keys, ref_values):
    head_width = queries.shape[1]
    frames = queries.shape[0] // FT
    groups = frames // 2
    key_pairs = key_rows.reshape(groups + 1, 2 * FT, head_width)
    val_pairs = values.reshape(groups + 1, 2 * FT, head_width)
    key_window = jnp.concatenate([key_pairs[:-1], key_pairs[1:]], axis=1)
    val_window = jnp.concatenate([val_pairs[:-1], val_pairs[1:]], axis=1)
    query_groups = queries.reshape(groups, 2 * FT, head_width)
    row_frame = (jnp.arange(2 * FT) // FT)[:, None]
    col_frame = (jnp.arange(4 * FT) // FT)[None, :]
    offset = col_frame - row_frame
    in_window = jnp.logical_and(offset >= 0, offset <= 2)
    scale = 1.0 / head_width ** 0.5

    def one_group(inputs):
        group_q, group_k, group_v, group_id = inputs
        first_ok = jnp.logical_or(group_id > 0, has_prev)
        last_ok = jnp.logical_or(group_id < groups - 1, has_next)
        edge_ok = jnp.logical_and(jnp.logical_or(col_frame != 0, first_ok), jnp.logical_or(col_frame != 3, last_ok))
        allowed = jnp.logical_and(in_window, edge_ok)
        local_scores = jnp.dot(group_q, group_k.T, preferred_element_type=jnp.float32) * scale
        local_scores = jnp.where(allowed, local_scores, far_below)
        remote = jnp.dot(group_q, ref_keys.T, preferred_element_type=jnp.float32) * scale
        row_max = jnp.maximum(lax.optimization_barrier(jnp.max(local_scores, axis=1)), lax.optimization_barrier(jnp.max(remote, axis=1)))[:, None]
        probs_local = jnp.exp(local_scores - row_max)
        probs_remote = jnp.exp(remote - row_max)
        denominator = (lax.optimization_barrier(jnp.sum(probs_local, axis=1)) + lax.optimization_barrier(jnp.sum(probs_remote, axis=1)))[:, None]
        weight_local = (probs_local / denominator).astype(jnp.bfloat16)
        weight_remote = (probs_remote / denominator).astype(jnp.bfloat16)
        result = jnp.dot(weight_local, group_v, preferred_element_type=jnp.float32)
        result = result + jnp.dot(weight_remote, ref_values, preferred_element_type=jnp.float32)
        return result.astype(jnp.bfloat16)
    results = lax.map(one_group, (query_groups, key_window, val_window, jnp.arange(groups)))
    return results.reshape(groups * 2 * FT, head_width)

def reference(state, fresh, frame_level, request, q_table, k_table, step_size, reference_kv):
    block_len = FRAMES * FT
    current = state.reshape(N_QUEUE, block_len, HD)
    block_ids = jnp.arange(N_QUEUE)
    for sweep in range(ITERS):
        levels = frame_level[sweep].reshape(N_QUEUE, FRAMES)

        def project(block_id):
            as_float = current[block_id].astype(jnp.float32)
            row_scale = lax.rsqrt(lax.optimization_barrier(jnp.mean(as_float * as_float, axis=1)) + epsilon)
            token_level = jnp.repeat(levels[block_id], FT)
            normed = as_float * row_scale[:, None]
            queries = (normed * q_table[token_level]).astype(jnp.bfloat16)
            key_rows = (normed * k_table[token_level]).astype(jnp.bfloat16)
            return (queries, key_rows)
        all_queries, all_keys = lax.map(project, block_ids)

        def attend(block_id):
            prev_id = jnp.maximum(block_id - 1, 0)
            next_id = jnp.minimum(block_id + 1, N_QUEUE - 1)
            key_pad = jnp.concatenate([all_keys[prev_id][block_len - FT:], all_keys[block_id], all_keys[next_id][:FT]], axis=0)
            val_pad = jnp.concatenate([current[prev_id][block_len - FT:], current[block_id], current[next_id][:FT]], axis=0)
            chosen = request[sweep, block_id]
            ref_keys = reference_kv[0, chosen]
            ref_values = reference_kv[1, chosen]
            per_head = jax.vmap(frame_attention, in_axes=(1, 1, 1, None, None, 1, 1), out_axes=1)
            attn = per_head(all_queries[block_id].reshape(block_len, HEADS, HDIM), key_pad.reshape(block_len + 2 * FT, HEADS, HDIM), val_pad.reshape(block_len + 2 * FT, HEADS, HDIM), block_id > 0, block_id < N_QUEUE - 1, ref_keys.reshape(FT, HEADS, HDIM), ref_values.reshape(FT, HEADS, HDIM))
            attn = attn.reshape(block_len, HD)
            step_rows = jnp.repeat(step_size[levels[block_id]], FT)
            updated = current[block_id].astype(jnp.float32) + step_rows[:, None] * attn.astype(jnp.float32)
            return updated.astype(jnp.bfloat16)
        current = lax.map(attend, block_ids)
        if sweep < ITERS - 1:
            current = jnp.concatenate([fresh[sweep][None], current[:-1]], axis=0)
    return current.reshape(TOKENS, HD)
```

```python
import functools
import math

import jax
import jax.numpy as jnp
from jax import lax
from jax.experimental import pallas as pl
from jax.experimental.pallas import tpu as pltpu
from jax.sharding import PartitionSpec as P

FT = 256
FRAMES = 16
HALF = 128
HD = 4096
WIDTH = 128
QUEUE = 16
PLANE = 16
ROWS = 128

epsilon = 1e-06
far_below = -1e30
MESH = pl.DeviceIdType.MESH
HIGHEST = lax.Precision.HIGHEST
BF16 = jnp.bfloat16
F32 = jnp.float32


def dot_nt(a, b, precision=None):
    return lax.dot_general(
        a, b, (((1,), (1,)), ((), ())), precision=precision, preferred_element_type=F32
    )


def slot(index):
    return pl.ds(pl.multiple_of(index * FT, FT), FT)


def half_rows(index):
    return pl.ds(pl.multiple_of(index * HALF, HALF), HALF)


def columns(head):
    return pl.ds(pl.multiple_of(head * WIDTH, WIDTH), WIDTH)


def kernel(
    state, fresh, meta, q_tab, k_tab, step_tab, ref_kv,
    out,
    src, cross, fresh0, fresh0_cross,
    x0, k0, x1, k1, qs, ys, back,
    r_in, r_rows, r_full, sums, sums_other, sums_both, sums_all,
    meta_next, tables, q_scale, k_scale, step_rows, ref_k, ref_v,
    s_cross, r_cross, s_stay, r_stay, s_row, r_row, s_z, r_z, s_zrow, r_zrow,
    s_halo, r_halo, s_meta, r_meta, s_sum, r_sum, s_all, r_all,
    s_back, r_back, s_out, r_out, s_f, r_f, s_fc, r_fc, s_fz, r_fz,
):
    q = lax.axis_index("queue")
    h = lax.axis_index("heads")
    z_hi = (h // 4) % 2
    me = (h // 8) * 4 + h % 4
    other = h + 4 - 8 * z_hi
    q_next = (q + 1) % QUEUE
    q_prev = (q + QUEUE - 1) % QUEUE
    last = q == QUEUE - 1

    def head_of(place, part):
        return (place // 4) * 8 + part * 4 + place % 4

    def remote(a, b, send, recv, to_q, to_h):
        return pltpu.make_async_remote_copy(
            src_ref=a, dst_ref=b, send_sem=send, recv_sem=recv,
            device_id=(to_q, to_h), device_id_type=MESH,
        )

    def own_frame(i):
        flip = ((i // 2) + z_hi) % 2
        return i + flip * (15 - 2 * i)

    def compact(frame):
        return (frame // 4) * 2 + frame % 2

    barrier = pltpu.get_barrier_semaphore()

    def greet(to_q, to_h):
        pl.semaphore_signal(barrier, inc=1, device_id=(to_q, to_h), device_id_type=MESH)

    greet(q, other)
    greet(q_next, other)
    greet(q_prev, other)
    greet(q_next, h)
    greet(q_prev, h)

    @pl.loop(1, PLANE)
    def _(k):
        greet(q, head_of((me + k) % PLANE, z_hi))

    holds_first = jnp.logical_and(h // 8 == 0, jnp.logical_and(z_hi == 0, h % 4 < 2))
    use_fresh = jnp.logical_and(last, jnp.logical_not(holds_first))

    @pl.when(use_fresh)
    def _():
        src[...] = fresh[...]

    @pl.when(jnp.logical_not(use_fresh))
    def _():
        src[...] = state[...]

    total = jnp.zeros((HALF, WIDTH), F32)
    for block in range(HD // WIDTH):
        part = src[:, block * WIDTH : (block + 1) * WIDTH].astype(F32)
        total = total + part * part
    ones = jnp.ones((8, WIDTH), F32)
    own_row = lax.rsqrt(dot_nt(ones, total, HIGHEST) / HD + epsilon)

    def modulation(sweep, table_of):
        levels = table_of[0:FRAMES, :]
        lanes = lax.broadcasted_iota(jnp.int32, (FRAMES, 128), 1)
        one_hot = (levels == lanes).astype(F32)
        for table, result in ((0, q_scale), (1, k_scale)):
            result[sweep] = lax.dot_general(
                one_hot, tables[table], (((1,), (0,)), ((), ())),
                precision=HIGHEST, preferred_element_type=F32,
            )
        picked = jnp.sum(one_hot * step_tab[...], axis=1, keepdims=True)
        step_rows[sweep] = jnp.broadcast_to(picked, (FRAMES, WIDTH))
        wanted = table_of[FRAMES : FRAMES + 1, :]
        for part, result in ((0, ref_k), (1, ref_v)):
            chosen = jnp.zeros((FT, WIDTH), F32)
            for request in range(ref_kv.shape[1]):
                chosen = jnp.where(wanted == request, ref_kv[part, request].astype(F32), chosen)
            result[sweep] = chosen.astype(BF16)

    tables[...] = jnp.zeros_like(tables)
    tables[0, 0:48, :] = q_tab[...]
    tables[1, 0:48, :] = k_tab[...]
    modulation(0, meta.at[0])

    r_in[me] = own_row
    pl.semaphore_wait(barrier, PLANE - 1 + 5)

    def row_copy(place):
        return remote(r_in.at[me], r_in.at[me], s_row.at[place], r_row.at[me], q, head_of(place, z_hi))

    def cross_copy(place):
        return remote(
            src.at[:, columns(head_of(place, 1 - z_hi))], cross.at[half_rows(me)],
            s_cross.at[place], r_cross.at[me], q, head_of(place, z_hi),
        )

    def stay_rows(place):
        return half_rows(2 + (place // 4) * 8 + z_hi * 4 + place % 4)

    def stay_copy(place):
        return remote(
            src.at[:, columns(head_of(place, z_hi))], x0.at[stay_rows(me)],
            s_stay.at[place], r_stay.at[me], q, head_of(place, z_hi),
        )

    @pl.loop(1, PLANE)
    def _(k):
        row_copy((me + k) % PLANE).start()

    own_cross = pltpu.make_async_copy(
        src.at[:, columns(other)], cross.at[half_rows(me)], r_cross.at[me]
    )
    own_cross.start()

    @pl.loop(1, PLANE)
    def _(k):
        cross_copy((me + k) % PLANE).start()

    own_stay = pltpu.make_async_copy(src.at[:, columns(h)], x0.at[stay_rows(me)], r_stay.at[me])
    own_stay.start()

    @pl.loop(1, PLANE)
    def _(k):
        stay_copy((me + k) % PLANE).start()

    meta_copy = remote(meta.at[1], meta_next, s_meta, r_meta, q_prev, h)
    meta_copy.start()

    def fresh0_copy(place, crossing):
        half = h % 4
        part = z_hi + crossing * (1 - 2 * z_hi)
        target = fresh0_cross if crossing else fresh0
        send, recv = (s_fc, r_fc) if crossing else (s_f, r_f)
        return remote(
            fresh.at[:, columns(head_of(place, part))], target.at[half_rows(half)],
            send.at[place], recv.at[half], q, head_of(place, z_hi),
        )

    gives_fresh0 = jnp.logical_and(last, holds_first)

    @pl.when(gives_fresh0)
    def _():
        half = h % 4
        pltpu.make_async_copy(
            fresh.at[:, columns(other)], fresh0_cross.at[half_rows(half)], r_fc.at[half]
        ).start()
        pltpu.make_async_copy(
            fresh.at[:, columns(h)], fresh0.at[half_rows(half)], r_f.at[half]
        ).start()

        @pl.loop(1, PLANE)
        def _(k):
            fresh0_copy((me + k) % PLANE, 1).start()
            fresh0_copy((me + k) % PLANE, 0).start()

    def wait_bytes(ref, sem):
        pltpu.make_async_copy(ref, ref, sem).wait()

    @pl.loop(1, PLANE)
    def _(k):
        place = (me + k) % PLANE
        wait_bytes(r_in.at[place], r_row.at[place])

    for place in range(PLANE):
        r_rows[z_hi, place : place + 1, :] = r_in[place, 0:1, :]
    zrow_copy = remote(r_rows.at[z_hi], r_rows.at[z_hi], s_zrow, r_zrow, q, other)
    zrow_copy.start()

    def z_copy(i):
        frame = own_frame(i)
        return remote(
            cross.at[slot(compact(frame))], x0.at[slot(frame + 1)], s_z.at[i], r_z.at[i], q, other
        )

    def send_z(i):
        c = compact(own_frame(i))
        wait_bytes(cross.at[half_rows(2 * c)], r_cross.at[2 * c])
        wait_bytes(cross.at[half_rows(2 * c + 1)], r_cross.at[2 * c + 1])
        z_copy(i).start()

    @pl.loop(0, 2)
    def _(i):
        send_z(i)

    fresh0_z = remote(fresh0_cross, fresh0, s_fz, r_fz, q, other)
    relays_fresh0 = jnp.logical_and(last, z_hi == 0)
    takes_fresh0 = jnp.logical_and(last, z_hi == 1)

    @pl.when(relays_fresh0)
    def _():
        for half in range(2):
            wait_bytes(fresh0_cross.at[half_rows(half)], r_fc.at[half])
        fresh0_z.start()

    @pl.loop(2, 8)
    def _(i):
        send_z(i)

    def spread(rows_value, count, target_rows):
        padded = jnp.concatenate(
            [rows_value, jnp.zeros((128 - rows_value.shape[0], 128), F32)], axis=0
        )
        turned = jnp.transpose(padded)
        for index in range(count):
            r_full[target_rows(index), :] = jnp.broadcast_to(turned[:, index : index + 1], (128, 128))

    wait_bytes(r_rows.at[1 - z_hi], r_zrow)

    def first_rows(index):
        part, place = index // PLANE, index % PLANE
        chunk = (place // 4) * 8 + part * 4 + place % 4
        return half_rows(chunk)

    spread(jnp.concatenate([r_rows[0], r_rows[1]], axis=0), 2 * PLANE, first_rows)

    def prepare(sweep, x_ref, k_ref, frame):
        normed = x_ref[slot(frame + 1), :].astype(F32) * r_full[slot(frame), :]
        qs[slot(frame), :] = (normed * q_scale[sweep, pl.ds(frame, 1), :]).astype(BF16)
        k_ref[slot(frame + 1), :] = (normed * k_scale[sweep, pl.ds(frame, 1), :]).astype(BF16)

    factor = math.log2(math.e) / math.sqrt(WIDTH)

    def attend(sweep, x_ref, k_ref, frame, no_prev, no_next, target, target_slot):
        before = jnp.where(jnp.logical_and(frame == 0, no_prev), far_below, 0.0).astype(F32)
        after = jnp.where(jnp.logical_and(frame == FRAMES - 1, no_next), far_below, 0.0).astype(F32)
        step = step_rows[sweep, pl.ds(frame, 1), :]

        @pl.loop(0, FT // ROWS)
        def _(chunk):
            start = pl.multiple_of(frame * FT + chunk * ROWS, ROWS)
            query = qs[pl.ds(start, ROWS), :]
            scores = []
            for part in range(3):
                scores.append(dot_nt(query, k_ref[slot(frame + part), :]))
            scores[0] = scores[0] + before
            scores[2] = scores[2] + after
            scores.append(dot_nt(query, ref_k[sweep]))
            high = jnp.maximum(
                jnp.maximum(scores[0], scores[1]), jnp.maximum(scores[2], scores[3])
            )
            high = jnp.max(high, axis=1, keepdims=True)
            probs = [jnp.exp2((part - high) * factor) for part in scores]
            weight = (probs[0] + probs[1]) + (probs[2] + probs[3])
            weight = jnp.sum(weight, axis=1, keepdims=True)
            result = jnp.dot(probs[3].astype(BF16), ref_v[sweep], preferred_element_type=F32)
            for part in range(3):
                result = result + jnp.dot(
                    probs[part].astype(BF16), x_ref[slot(frame + part), :],
                    preferred_element_type=F32,
                )
            attn = (result / weight).astype(BF16).astype(F32)
            held = x_ref[pl.ds(start + FT, ROWS), :].astype(F32)
            place = pl.multiple_of(target_slot * FT + chunk * ROWS, ROWS)
            target[pl.ds(place, ROWS), :] = (held + step * attn).astype(BF16)

    def halo_copies(sweep, x_ref, k_ref):
        copies = []
        for index, (ref, here, there, to_q) in enumerate((
            (k_ref, 1, 17, q_prev), (x_ref, 1, 17, q_prev),
            (k_ref, 16, 0, q_next), (x_ref, 16, 0, q_next),
        )):
            copies.append(remote(
                ref.at[slot(here)], ref.at[slot(there)],
                s_halo.at[sweep, index], r_halo.at[sweep, index], to_q, h,
            ))
        return copies

    def start_halo(sweep, x_ref, k_ref):
        for copy in halo_copies(sweep, x_ref, k_ref):
            copy.start()

    def wait_halo(sweep, x_ref, k_ref):
        for copy in halo_copies(sweep, x_ref, k_ref):
            copy.wait_recv()

    def arrive(i):
        frame = own_frame(i)
        c = compact(frame)
        for half in range(2):
            wait_bytes(x0.at[half_rows(2 * (frame + 1) + half)], r_stay.at[2 * c + half])
        wait_bytes(x0.at[slot(16 - frame)], r_z.at[i])

    def first_pairs(i0, count):
        @pl.loop(0, 2 * count)
        def _(k):
            i = i0 + k // 2
            frame = i + (k % 2) * (15 - 2 * i)
            attend(0, x0, k0, frame, q == 0, last, x1, frame + 1)

            @pl.when(last)
            def _():
                x1[slot(frame + 1), :] = x0[slot(frame + 1), :]

    def take_fresh0():
        @pl.when(jnp.logical_and(last, z_hi == 0))
        def _():
            for half in range(2):
                wait_bytes(fresh0.at[half_rows(half)], r_f.at[half])

        @pl.when(takes_fresh0)
        def _():
            wait_bytes(fresh0, r_fz)

        @pl.when(last)
        def _():
            x1[slot(1), :] = fresh0[...]

    def sum_copy(group):
        return remote(
            sums.at[group], sums_other.at[group], s_sum.at[group], r_sum.at[group], q, other
        )

    def start_sums(group):
        for index in range(4):
            i = 2 * group + index // 2
            frame = i if index % 2 == 0 else 15 - i
            held = x1[slot(frame + 1), :].astype(F32)
            row = dot_nt(ones, held * held, HIGHEST)
            sums[group, 2 * index : 2 * index + 1, :] = row[0:1, 0:128]
            sums[group, 2 * index + 1 : 2 * index + 2, :] = row[0:1, 128:256]
        sum_copy(group).start()

    def all_copy(group, place):
        return remote(
            sums_both.at[group], sums_all.at[group, me],
            s_all.at[group, place], r_all.at[group, me], q, head_of(place, z_hi),
        )

    def spread_sums(group):
        wait_bytes(sums_other.at[group], r_sum.at[group])
        both = sums[group] + sums_other[group]
        sums_both[group] = both

        @pl.loop(1, PLANE)
        def _(k):
            all_copy(group, (me + k) % PLANE).start()

        sums_all[group, me] = both

    def prepare_group(group):
        @pl.loop(1, PLANE)
        def _(k):
            place = (me + k) % PLANE
            wait_bytes(sums_all.at[group, place], r_all.at[group, place])

        whole = sums_all[group, 0]
        for place in range(1, PLANE):
            whole = whole + sums_all[group, place]
        rows = lax.rsqrt(whole / HD + epsilon)

        def group_rows(index):
            i = 2 * group + index // 4
            frame = i if (index // 2) % 2 == 0 else 15 - i
            return half_rows(2 * frame + index % 2)

        spread(rows, 8, group_rows)

        @pl.loop(0, 4)
        def _(k):
            i = 2 * group + k // 2
            prepare(1, x1, k1, i + (k % 2) * (15 - 2 * i))

    def back_copy(frame):
        moves = ((frame // 2) + z_hi) % 2
        return remote(
            ys.at[slot(frame)], back.at[moves, slot(compact(frame))],
            s_back.at[frame], r_back.at[moves, compact(frame)],
            q_next, h + moves * (4 - 8 * z_hi),
        )

    def second_pairs(i0, count):
        @pl.loop(0, 2 * count)
        def _(k):
            i = i0 + k // 2
            frame = i + (k % 2) * (15 - 2 * i)
            attend(1, x1, k1, frame, last, q == QUEUE - 2, ys, frame)
            back_copy(frame).start()

    def prepare_pair(i):
        @pl.loop(0, 2)
        def _(k):
            prepare(0, x0, k0, i + k * (15 - 2 * i))

    arrive(0)
    prepare_pair(0)
    start_halo(0, x0, k0)
    arrive(1)
    prepare_pair(1)
    wait_halo(0, x0, k0)
    first_pairs(0, 1)
    take_fresh0()
    arrive(2)
    prepare_pair(2)
    first_pairs(1, 1)
    start_sums(0)
    wait_bytes(meta_next, r_meta)
    modulation(1, meta_next)
    arrive(3)
    prepare_pair(3)
    first_pairs(2, 1)
    spread_sums(0)
    arrive(4)
    prepare_pair(4)
    first_pairs(3, 1)
    start_sums(1)
    arrive(5)
    prepare_pair(5)
    first_pairs(4, 1)
    spread_sums(1)
    arrive(6)
    prepare_pair(6)
    first_pairs(5, 1)
    start_sums(2)
    arrive(7)
    prepare_pair(7)
    first_pairs(6, 2)
    start_sums(3)
    prepare_group(0)
    start_halo(1, x1, k1)
    prepare_group(1)
    wait_halo(1, x1, k1)
    second_pairs(0, 1)
    second_pairs(1, 2)
    spread_sums(2)
    prepare_group(2)
    second_pairs(3, 2)
    spread_sums(3)
    prepare_group(3)
    second_pairs(5, 3)

    def out_copy(part, c, half):
        place = 2 * c + half
        head = h + part * (4 - 8 * z_hi)
        return remote(
            back.at[part, half_rows(place)], out.at[:, columns(head)],
            s_out.at[part, place], r_out.at[part, me], q, head_of(place, z_hi),
        )

    def out_local(part):
        head = h + part * (4 - 8 * z_hi)
        return pltpu.make_async_copy(
            back.at[part, half_rows(me)], out.at[:, columns(head)], r_out.at[part, me]
        )

    @pl.loop(0, 16)
    def _(k):
        c = compact(own_frame(k // 2))
        part = k % 2
        wait_bytes(back.at[part, slot(c)], r_back.at[part, c])
        for half in range(2):
            place = 2 * c + half

            @pl.when(place == me)
            def _():
                out_local(part).start()

            @pl.when(place != me)
            def _():
                out_copy(part, c, half).start()

    @pl.loop(0, 2 * PLANE)
    def _(k):
        part, place = k // PLANE, k % PLANE
        head = head_of(place, z_hi + part - 2 * z_hi * part)
        wait_bytes(out.at[:, columns(head)], r_out.at[part, place])

    @pl.loop(1, PLANE)
    def _(k):
        place = (me + k) % PLANE
        row_copy(place).wait_send()
        cross_copy(place).wait_send()
        stay_copy(place).wait_send()
        for part in range(2):
            out_copy(part, place // 2, place % 2).wait_send()
        for group in range(4):
            all_copy(group, place).wait_send()

    @pl.when(gives_fresh0)
    def _():
        @pl.loop(1, PLANE)
        def _(k):
            fresh0_copy((me + k) % PLANE, 1).wait_send()
            fresh0_copy((me + k) % PLANE, 0).wait_send()

    @pl.when(relays_fresh0)
    def _():
        fresh0_z.wait_send()

    meta_copy.wait_send()
    zrow_copy.wait_send()

    @pl.loop(0, 8)
    def _(i):
        z_copy(i).wait_send()

    for group in range(4):
        sum_copy(group).wait_send()
    for sweep, (x_ref, k_ref) in enumerate(((x0, k0), (x1, k1))):
        for copy in halo_copies(sweep, x_ref, k_ref):
            copy.wait_send()

    @pl.loop(0, FRAMES)
    def _(frame):
        back_copy(frame).wait_send()


def local(state, fresh, frame_level, request, q_table, k_table, step_size, reference_kv):
    meta = jnp.concatenate(
        [
            jnp.broadcast_to(frame_level[:, :, None], (2, FRAMES, 128)),
            jnp.broadcast_to(request[:, :, None], (2, 8, 128)),
        ],
        axis=1,
    )
    step_tab = jnp.pad(step_size, (0, 128 - step_size.shape[0]))[None, :]
    block = FRAMES * FT
    dma = pltpu.SemaphoreType.DMA
    vmem = pl.BlockSpec(memory_space=pltpu.VMEM)
    return pl.pallas_call(
        kernel,
        out_shape=jax.ShapeDtypeStruct(state.shape, state.dtype),
        in_specs=[vmem] * 7,
        out_specs=vmem,
        scratch_shapes=[
            pltpu.VMEM((HALF, HD), BF16),
            pltpu.VMEM((block // 2, WIDTH), BF16),
            pltpu.VMEM((FT, WIDTH), BF16),
            pltpu.VMEM((FT, WIDTH), BF16),
            pltpu.VMEM((block + 2 * FT, WIDTH), BF16),
            pltpu.VMEM((block + 2 * FT, WIDTH), BF16),
            pltpu.VMEM((block + 2 * FT, WIDTH), BF16),
            pltpu.VMEM((block + 2 * FT, WIDTH), BF16),
            pltpu.VMEM((block, WIDTH), BF16),
            pltpu.VMEM((block, WIDTH), BF16),
            pltpu.VMEM((2, block // 2, WIDTH), BF16),
            pltpu.VMEM((PLANE, 8, 128), F32),
            pltpu.VMEM((2, PLANE, 128), F32),
            pltpu.VMEM((block, 128), F32),
            pltpu.VMEM((4, 8, 128), F32),
            pltpu.VMEM((4, 8, 128), F32),
            pltpu.VMEM((4, 8, 128), F32),
            pltpu.VMEM((4, PLANE, 8, 128), F32),
            pltpu.VMEM((24, 128), jnp.int32),
            pltpu.VMEM((2, 128, WIDTH), F32),
            pltpu.VMEM((2, FRAMES, WIDTH), F32),
            pltpu.VMEM((2, FRAMES, WIDTH), F32),
            pltpu.VMEM((2, FRAMES, WIDTH), F32),
            pltpu.VMEM((2, FT, WIDTH), BF16),
            pltpu.VMEM((2, FT, WIDTH), BF16),
            dma((PLANE,)), dma((PLANE,)), dma((PLANE,)), dma((PLANE,)), dma((PLANE,)), dma((PLANE,)),
            dma((8,)), dma((8,)), dma, dma,
            dma((2, 4)), dma((2, 4)), dma, dma, dma((4,)), dma((4,)), dma((4, PLANE)), dma((4, PLANE)),
            dma((FRAMES,)), dma((2, 8)), dma((2, PLANE)), dma((2, PLANE)),
            dma((PLANE,)), dma((2,)), dma((PLANE,)), dma((2,)), dma, dma,
        ],
        compiler_params=pltpu.CompilerParams(
            collective_id=0, has_side_effects=True, vmem_limit_bytes=48 << 20
        ),
    )(state, fresh[0], meta, q_table, k_table, step_tab, reference_kv)


def solution(mesh):
    placed = (
        P(("queue", "heads"), None),
        P(None, "heads", None),
        P(None, "queue"),
        P(None, "queue"),
        P(None, "heads"),
        P(None, "heads"),
        P(),
        P(None, None, None, "heads"),
    )
    return jax.shard_map(
        local, mesh=mesh, in_specs=placed, out_specs=P(("queue", "heads"), None), check_vma=False
    )
```

```python
import functools
import math

import jax
import jax.numpy as jnp
from jax import lax
from jax.experimental import pallas as pl
from jax.experimental.pallas import tpu as pltpu
from jax.sharding import PartitionSpec as P

FT = 256
FRAMES = 16
HALF = 128
HD = 4096
WIDTH = 128
QUEUE = 16
PLANE = 16
ROWS = 256
RELAYED = 6

epsilon = 1e-06
far_below = -1e30
MESH = pl.DeviceIdType.MESH
HIGHEST = lax.Precision.HIGHEST
BF16 = jnp.bfloat16
F32 = jnp.float32


def dot_nt(a, b, precision=None):
    return lax.dot_general(
        a, b, (((1,), (1,)), ((), ())), precision=precision, preferred_element_type=F32
    )


def slot(index):
    return pl.ds(pl.multiple_of(index * FT, FT), FT)


def half_rows(index):
    return pl.ds(pl.multiple_of(index * HALF, HALF), HALF)


def columns(head):
    return pl.ds(pl.multiple_of(head * WIDTH, WIDTH), WIDTH)


def kernel(
    state, fresh, frame_level, request, q_tab, k_tab, step_size, ref_in,
    out,
    src, cross, fresh0, fresh0_cross,
    x0, k0, x1, k1, qs, ys, back,
    r_in, r_rows, r_full, sums, sums_other, sums_both, sums_all,
    levels, levels_next, wanted, wanted_next, tables, step_tab, ref_kv, level_pad,
    q_scale, k_scale, step_rows, ref_k, ref_v,
    s_cross, r_cross, s_stay, r_stay, s_row, r_row, s_z, r_z, s_zrow, r_zrow,
    s_halo, r_halo, s_meta, r_meta, s_sum, r_sum, s_all, r_all,
    s_back, r_back, s_out, r_out, s_f, r_f, s_fc, r_fc, s_fz, r_fz,
    load, via, s_via, r_via,
):
    q = lax.axis_index("queue")
    h = lax.axis_index("heads")
    z_hi = (h // 4) % 2
    me = (h // 8) * 4 + h % 4
    other = h + 4 - 8 * z_hi
    q_next = (q + 1) % QUEUE
    q_prev = (q + QUEUE - 1) % QUEUE
    last = q == QUEUE - 1

    def head_of(place, part):
        return (place // 4) * 8 + part * 4 + place % 4

    def remote(a, b, send, recv, to_q, to_h):
        return pltpu.make_async_remote_copy(
            src_ref=a, dst_ref=b, send_sem=send, recv_sem=recv,
            device_id=(to_q, to_h), device_id_type=MESH,
        )

    def own_frame(i):
        flip = ((i // 2) + z_hi) % 2
        return i + flip * (15 - 2 * i)

    def compact(frame):
        return (frame // 4) * 2 + frame % 2

    barrier = pltpu.get_barrier_semaphore()

    def greet(to_q, to_h):
        pl.semaphore_signal(barrier, inc=1, device_id=(to_q, to_h), device_id_type=MESH)

    greet(q, other)
    greet(q_next, other)
    greet(q_prev, other)
    greet(q_next, h)
    greet(q_prev, h)

    relays_fresh0 = jnp.logical_and(q == 1, z_hi == 0)
    takes_fresh0 = jnp.logical_and(last, z_hi == 1)

    @pl.when(relays_fresh0)
    def _():
        greet(QUEUE - 1, other)

    @pl.when(takes_fresh0)
    def _():
        greet(1, other)


    @pl.loop(1, PLANE)
    def _(k):
        greet(q, head_of((me + k) % PLANE, z_hi))

    holds_first = jnp.logical_and(h // 8 == 0, jnp.logical_and(z_hi == 0, h % 4 < 2))
    use_fresh = jnp.logical_and(last, jnp.logical_not(holds_first))

    @pl.when(use_fresh)
    def _():
        pltpu.make_async_copy(fresh, src, load.at[0]).start()

    @pl.when(jnp.logical_not(use_fresh))
    def _():
        pltpu.make_async_copy(state, src, load.at[0]).start()

    tables[...] = jnp.zeros_like(tables)
    loads = [
        pltpu.make_async_copy(a, b, load.at[1 + index])
        for index, (a, b) in enumerate((
            (frame_level, levels), (request, wanted), (step_size, step_tab),
            (q_tab, tables.at[0, 0:48]), (k_tab, tables.at[1, 0:48]), (ref_in, ref_kv),
        ))
    ]
    for copy in loads:
        copy.start()
    pltpu.make_async_copy(state, src, load.at[0]).wait()

    total = jnp.zeros((HALF, WIDTH), F32)
    for block in range(HD // WIDTH):
        part = src[:, block * WIDTH : (block + 1) * WIDTH].astype(F32)
        total = total + part * part
    ones = jnp.ones((8, WIDTH), F32)
    own_row = lax.rsqrt(dot_nt(ones, total, HIGHEST) / HD + epsilon)

    def modulation(sweep, level_ref, wanted_ref):
        level_pad[...] = jnp.zeros_like(level_pad)
        level_pad[0:2, 0:FRAMES] = level_ref[...].astype(F32)
        turned = jnp.transpose(level_pad[...])
        own = turned[0:FRAMES, sweep : sweep + 1]
        lanes = lax.broadcasted_iota(jnp.int32, (FRAMES, 128), 1).astype(F32)
        one_hot = (jnp.broadcast_to(own, (FRAMES, 128)) == lanes).astype(F32)
        for table, result in ((0, q_scale), (1, k_scale)):
            result[sweep] = lax.dot_general(
                one_hot, tables[table], (((1,), (0,)), ((), ())),
                precision=HIGHEST, preferred_element_type=F32,
            )
        picked = jnp.sum(one_hot[:, 0:48] * step_tab[...], axis=1, keepdims=True)
        step_rows[sweep] = jnp.broadcast_to(picked, (FRAMES, WIDTH))
        choice = jnp.broadcast_to(wanted_ref[sweep : sweep + 1, :], (FT, WIDTH))
        for part, result in ((0, ref_k), (1, ref_v)):
            chosen = jnp.zeros((FT, WIDTH), F32)
            for index in range(ref_kv.shape[1]):
                chosen = jnp.where(choice == index, ref_kv[part, index].astype(F32), chosen)
            result[sweep] = chosen.astype(BF16)

    for copy in loads:
        copy.wait()
    modulation(0, levels, wanted)

    r_in[me] = own_row
    extra = jnp.logical_or(relays_fresh0, takes_fresh0).astype(jnp.int32)
    pl.semaphore_wait(barrier, PLANE - 1 + 5 + extra)

    def row_copy(place):
        return remote(r_in.at[me], r_in.at[me], s_row.at[place], r_row.at[me], q, head_of(place, z_hi))

    def cross_copy(place):
        return remote(
            src.at[:, columns(head_of(place, 1 - z_hi))], cross.at[half_rows(me)],
            s_cross.at[place], r_cross.at[me], q, head_of(place, z_hi),
        )

    def stay_rows(place):
        return half_rows(2 + (place // 4) * 8 + z_hi * 4 + place % 4)

    def stay_copy(place):
        return remote(
            src.at[:, columns(head_of(place, z_hi))], x0.at[stay_rows(me)],
            s_stay.at[place], r_stay.at[me], q, head_of(place, z_hi),
        )

    @pl.loop(1, PLANE)
    def _(k):
        row_copy((me + k) % PLANE).start()

    own_cross = pltpu.make_async_copy(
        src.at[:, columns(other)], cross.at[half_rows(me)], r_cross.at[me]
    )
    own_cross.start()

    @pl.loop(1, PLANE)
    def _(k):
        cross_copy((me + k) % PLANE).start()

    own_stay = pltpu.make_async_copy(src.at[:, columns(h)], x0.at[stay_rows(me)], r_stay.at[me])
    own_stay.start()

    @pl.loop(1, PLANE)
    def _(k):
        stay_copy((me + k) % PLANE).start()

    meta_copies = [
        remote(levels, levels_next, s_meta.at[0], r_meta.at[0], q_prev, h),
        remote(wanted, wanted_next, s_meta.at[1], r_meta.at[1], q_prev, h),
    ]
    for copy in meta_copies:
        copy.start()

    def fresh0_copy(place, crossing):
        half = h % 4
        part = z_hi + crossing * (1 - 2 * z_hi)
        target = fresh0_cross if crossing else fresh0
        send, recv = (s_fc, r_fc) if crossing else (s_f, r_f)
        return remote(
            fresh.at[:, columns(head_of(place, part))], target.at[half_rows(half)],
            send.at[place], recv.at[half], q, head_of(place, z_hi),
        )

    gives_fresh0 = jnp.logical_and(last, holds_first)
    gives_cross0 = jnp.logical_and(q == 1, holds_first)

    for gives, crossing, head, target, recv in (
        (gives_cross0, 1, other, fresh0_cross, r_fc), (gives_fresh0, 0, h, fresh0, r_f),
    ):
        @pl.when(gives)
        def _():
            half = h % 4
            pltpu.make_async_copy(
                fresh.at[:, columns(head)], target.at[half_rows(half)], recv.at[half]
            ).start()

            @pl.loop(1, PLANE)
            def _(k):
                fresh0_copy((me + k) % PLANE, crossing).start()

    def wait_bytes(ref, sem):
        pltpu.make_async_copy(ref, ref, sem).wait()

    @pl.loop(1, PLANE)
    def _(k):
        place = (me + k) % PLANE
        wait_bytes(r_in.at[place], r_row.at[place])

    for place in range(PLANE):
        r_rows[z_hi, place : place + 1, :] = r_in[place, 0:1, :]
    zrow_copy = remote(r_rows.at[z_hi], r_rows.at[z_hi], s_zrow, r_zrow, q, other)
    zrow_copy.start()

    def z_copy(i):
        frame = own_frame(i)
        return remote(
            cross.at[slot(compact(frame))], x0.at[slot(frame + 1)], s_z.at[i], r_z.at[i], q, other
        )

    def send_z(i):
        c = compact(own_frame(i))
        wait_bytes(cross.at[half_rows(2 * c)], r_cross.at[2 * c])
        wait_bytes(cross.at[half_rows(2 * c + 1)], r_cross.at[2 * c + 1])
        z_copy(i).start()

    fresh0_z = remote(fresh0_cross, fresh0, s_fz, r_fz, QUEUE - 1, other)

    def send_fresh0():
        @pl.when(relays_fresh0)
        def _():
            for half in range(2):
                wait_bytes(fresh0_cross.at[half_rows(half)], r_fc.at[half])
            fresh0_z.start()

    send_z(0)
    send_z(1)
    send_fresh0()

    def spread(rows_value, count, target_rows):
        padded = jnp.concatenate(
            [rows_value, jnp.zeros((128 - rows_value.shape[0], 128), F32)], axis=0
        )
        turned = jnp.transpose(padded)
        for index in range(count):
            r_full[target_rows(index), :] = jnp.broadcast_to(turned[:, index : index + 1], (128, 128))

    wait_bytes(r_rows.at[1 - z_hi], r_zrow)

    def first_rows(index):
        part, place = index // PLANE, index % PLANE
        chunk = (place // 4) * 8 + part * 4 + place % 4
        return half_rows(chunk)

    spread(jnp.concatenate([r_rows[0], r_rows[1]], axis=0), 2 * PLANE, first_rows)

    def prepare(sweep, x_ref, k_ref, frame):
        normed = x_ref[slot(frame + 1), :].astype(F32) * r_full[slot(frame), :]
        qs[slot(frame), :] = (normed * q_scale[sweep, pl.ds(frame, 1), :]).astype(BF16)
        k_ref[slot(frame + 1), :] = (normed * k_scale[sweep, pl.ds(frame, 1), :]).astype(BF16)

    factor = math.log2(math.e) / math.sqrt(WIDTH)

    def attend(sweep, x_ref, k_ref, frame, no_prev, no_next, target, target_slot):
        before = jnp.where(jnp.logical_and(frame == 0, no_prev), far_below, 0.0).astype(F32)
        after = jnp.where(jnp.logical_and(frame == FRAMES - 1, no_next), far_below, 0.0).astype(F32)
        step = step_rows[sweep, pl.ds(frame, 1), :]

        @pl.loop(0, FT // ROWS)
        def _(chunk):
            start = pl.multiple_of(frame * FT + chunk * ROWS, ROWS)
            query = qs[pl.ds(start, ROWS), :]
            scores = []
            for part in range(3):
                scores.append(dot_nt(query, k_ref[slot(frame + part), :]))
            scores[0] = scores[0] + before
            scores[2] = scores[2] + after
            scores.append(dot_nt(query, ref_k[sweep]))
            high = jnp.maximum(
                jnp.maximum(scores[0], scores[1]), jnp.maximum(scores[2], scores[3])
            )
            high = jnp.max(high, axis=1, keepdims=True)
            probs = [jnp.exp2((part - high) * factor) for part in scores]
            weight = (probs[0] + probs[1]) + (probs[2] + probs[3])
            weight = jnp.sum(weight, axis=1, keepdims=True)
            result = jnp.dot(probs[3].astype(BF16), ref_v[sweep], preferred_element_type=F32)
            for part in range(3):
                result = result + jnp.dot(
                    probs[part].astype(BF16), x_ref[slot(frame + part), :],
                    preferred_element_type=F32,
                )
            attn = (result / weight).astype(BF16).astype(F32)
            held = x_ref[pl.ds(start + FT, ROWS), :].astype(F32)
            place = pl.multiple_of(target_slot * FT + chunk * ROWS, ROWS)
            target[pl.ds(place, ROWS), :] = (held + step * attn).astype(BF16)

    def halo_copies(sweep, x_ref, k_ref):
        copies = []
        for index, (ref, here, there, to_q) in enumerate((
            (k_ref, 1, 17, q_prev), (x_ref, 1, 17, q_prev),
            (k_ref, 16, 0, q_next), (x_ref, 16, 0, q_next),
        )):
            copies.append(remote(
                ref.at[slot(here)], ref.at[slot(there)],
                s_halo.at[sweep, index], r_halo.at[sweep, index], to_q, h,
            ))
        return copies

    def halo_roles(sweep):
        if sweep == 0:
            return q != 0, q < QUEUE - 2, q != QUEUE - 1, jnp.logical_and(q != 0, q != QUEUE - 1)
        return q != QUEUE - 1, q != QUEUE - 2, q != QUEUE - 2, q != QUEUE - 1

    def start_halo(sweep, x_ref, k_ref):
        copies = halo_copies(sweep, x_ref, k_ref)
        to_prev, to_next, from_next, from_prev = halo_roles(sweep)
        for group, wanted_here in ((copies[:2], to_prev), (copies[2:], to_next)):
            @pl.when(wanted_here)
            def _():
                for copy in group:
                    copy.start()
        for rim, absent in ((17, jnp.logical_not(from_next)), (0, jnp.logical_not(from_prev))):
            @pl.when(absent)
            def _():
                for ref in (x_ref, k_ref):
                    ref[slot(rim), :] = jnp.zeros((FT, WIDTH), BF16)

    def wait_halo(sweep, x_ref, k_ref):
        copies = halo_copies(sweep, x_ref, k_ref)
        _, _, from_next, from_prev = halo_roles(sweep)
        for group, wanted_here in ((copies[:2], from_next), (copies[2:], from_prev)):
            @pl.when(wanted_here)
            def _():
                for copy in group:
                    copy.wait_recv()

    def wait_halo_sent(sweep, x_ref, k_ref):
        copies = halo_copies(sweep, x_ref, k_ref)
        to_prev, to_next, _, _ = halo_roles(sweep)
        for group, wanted_here in ((copies[:2], to_prev), (copies[2:], to_next)):
            @pl.when(wanted_here)
            def _():
                for copy in group:
                    copy.wait_send()

    def arrive(i):
        frame = own_frame(i)
        c = compact(frame)
        for half in range(2):
            wait_bytes(x0.at[half_rows(2 * (frame + 1) + half)], r_stay.at[2 * c + half])
        wait_bytes(x0.at[slot(16 - frame)], r_z.at[i])

    def first_pairs(i0, count):
        @pl.loop(0, 2 * count)
        def _(k):
            i = i0 + k // 2
            frame = i + (k % 2) * (15 - 2 * i)

            @pl.when(jnp.logical_not(last))
            def _():
                attend(0, x0, k0, frame, q == 0, last, x1, frame + 1)

            @pl.when(last)
            def _():
                x1[slot(frame + 1), :] = x0[slot(frame + 1), :]

    def take_fresh0():
        @pl.when(jnp.logical_and(last, z_hi == 0))
        def _():
            for half in range(2):
                wait_bytes(fresh0.at[half_rows(half)], r_f.at[half])

        @pl.when(takes_fresh0)
        def _():
            wait_bytes(fresh0, r_fz)

        @pl.when(last)
        def _():
            x1[slot(1), :] = fresh0[...]

    def sum_copy(group):
        return remote(
            sums.at[group], sums_other.at[group], s_sum.at[group], r_sum.at[group], q, other
        )

    def start_sums(group):
        for index in range(4):
            i = 2 * group + index // 2
            frame = i if index % 2 == 0 else 15 - i
            held = x1[slot(frame + 1), :].astype(F32)
            row = dot_nt(ones, held * held, HIGHEST)
            sums[group, 2 * index : 2 * index + 1, :] = row[0:1, 0:128]
            sums[group, 2 * index + 1 : 2 * index + 2, :] = row[0:1, 128:256]
        sum_copy(group).start()

    def all_copy(group, place):
        return remote(
            sums_both.at[group], sums_all.at[group, me],
            s_all.at[group, place], r_all.at[group, me], q, head_of(place, z_hi),
        )

    def spread_sums(group):
        wait_bytes(sums_other.at[group], r_sum.at[group])
        both = sums[group] + sums_other[group]
        sums_both[group] = both

        @pl.loop(1, PLANE)
        def _(k):
            all_copy(group, (me + k) % PLANE).start()

        sums_all[group, me] = both

    def prepare_group(group):
        @pl.loop(1, PLANE)
        def _(k):
            place = (me + k) % PLANE
            wait_bytes(sums_all.at[group, place], r_all.at[group, place])

        whole = sums_all[group, 0]
        for place in range(1, PLANE):
            whole = whole + sums_all[group, place]
        rows = lax.rsqrt(whole / HD + epsilon)

        def group_rows(index):
            i = 2 * group + index // 4
            frame = i if (index // 2) % 2 == 0 else 15 - i
            return half_rows(2 * frame + index % 2)

        spread(rows, 8, group_rows)

        @pl.loop(0, 4)
        def _(k):
            i = 2 * group + k // 2
            prepare(1, x1, k1, i + (k % 2) * (15 - 2 * i))

    def back_copy(frame):
        moves = ((frame // 2) + z_hi) % 2
        return remote(
            ys.at[slot(frame)], back.at[moves, slot(compact(frame))],
            s_back.at[frame], r_back.at[moves, compact(frame)],
            q_next, h + moves * (4 - 8 * z_hi),
        )

    def is_relayed(i, frame):
        moves = ((frame // 2) + z_hi) % 2
        far = jnp.where(last, 0, 1)
        return jnp.logical_and(q % 4 == 3, jnp.logical_and(moves == far, i < RELAYED))

    def via_copy(i, frame):
        near = h + jnp.where(last, 1, 0) * (4 - 8 * z_hi)
        return remote(
            ys.at[slot(frame)], via.at[slot(i)], s_back.at[frame], r_via.at[i], q_next, near
        )

    def onward_copy(i):
        c = compact(15 - own_frame(i))
        part = jnp.where(q == 0, 0, 1)
        return remote(
            via.at[slot(i)], back.at[part, slot(c)], s_via.at[i], r_back.at[part, c], q, other
        )

    def relay_back(i):
        @pl.when(q % 4 == 0)
        def _():
            wait_bytes(via.at[slot(i)], r_via.at[i])
            onward_copy(i).start()

    def second_pairs(i0, count):
        @pl.loop(0, 2 * count)
        def _(k):
            i = i0 + k // 2
            frame = i + (k % 2) * (15 - 2 * i)
            attend(1, x1, k1, frame, last, q == QUEUE - 2, ys, frame)

            @pl.when(is_relayed(i, frame))
            def _():
                via_copy(i, frame).start()

            @pl.when(jnp.logical_not(is_relayed(i, frame)))
            def _():
                back_copy(frame).start()

    def prepare_pair(i):
        @pl.loop(0, 2)
        def _(k):
            prepare(0, x0, k0, i + k * (15 - 2 * i))

    def next_z(i):
        z_copy(i - 2).wait_send()
        send_z(i)

    next_z(2)
    arrive(0)
    prepare_pair(0)
    start_halo(0, x0, k0)
    next_z(3)
    arrive(1)
    prepare_pair(1)
    wait_halo(0, x0, k0)
    first_pairs(0, 1)
    next_z(4)
    arrive(2)
    prepare_pair(2)
    first_pairs(1, 1)
    next_z(5)
    arrive(3)
    prepare_pair(3)
    first_pairs(2, 1)
    for index in range(2):
        meta_copies[index].wait_recv()
    modulation(1, levels_next, wanted_next)
    next_z(6)
    take_fresh0()
    start_sums(0)
    arrive(4)
    prepare_pair(4)
    first_pairs(3, 1)
    start_sums(1)
    next_z(7)
    spread_sums(0)
    arrive(5)
    prepare_pair(5)
    first_pairs(4, 1)
    spread_sums(1)
    prepare_group(0)
    start_halo(1, x1, k1)
    arrive(6)
    prepare_pair(6)
    first_pairs(5, 1)
    start_sums(2)
    wait_halo(1, x1, k1)
    second_pairs(0, 1)
    arrive(7)
    prepare_pair(7)
    first_pairs(6, 2)
    start_sums(3)
    prepare_group(1)
    second_pairs(1, 1)
    spread_sums(2)
    relay_back(0)
    second_pairs(2, 1)
    spread_sums(3)
    relay_back(1)
    prepare_group(2)
    second_pairs(3, 2)
    relay_back(2)
    prepare_group(3)
    second_pairs(5, 3)
    relay_back(3)
    relay_back(4)
    relay_back(5)

    def out_copy(part, c, half):
        place = 2 * c + half
        head = h + part * (4 - 8 * z_hi)
        return remote(
            back.at[part, half_rows(place)], out.at[:, columns(head)],
            s_out.at[part, place], r_out.at[part, me], q, head_of(place, z_hi),
        )

    def out_local(part):
        head = h + part * (4 - 8 * z_hi)
        return pltpu.make_async_copy(
            back.at[part, half_rows(me)], out.at[:, columns(head)], r_out.at[part, me]
        )

    @pl.loop(0, 16)
    def _(k):
        c = compact(own_frame(k // 2))
        part = k % 2
        wait_bytes(back.at[part, slot(c)], r_back.at[part, c])
        for half in range(2):
            place = 2 * c + half

            @pl.when(place == me)
            def _():
                out_local(part).start()

            @pl.when(place != me)
            def _():
                out_copy(part, c, half).start()

    @pl.loop(0, 2 * PLANE)
    def _(k):
        part, place = k // PLANE, k % PLANE
        head = head_of(place, z_hi + part - 2 * z_hi * part)
        wait_bytes(out.at[:, columns(head)], r_out.at[part, place])

    @pl.loop(1, PLANE)
    def _(k):
        place = (me + k) % PLANE
        row_copy(place).wait_send()
        cross_copy(place).wait_send()
        stay_copy(place).wait_send()
        for part in range(2):
            out_copy(part, place // 2, place % 2).wait_send()
        for group in range(4):
            all_copy(group, place).wait_send()

    for gives, crossing in ((gives_cross0, 1), (gives_fresh0, 0)):
        @pl.when(gives)
        def _():
            @pl.loop(1, PLANE)
            def _(k):
                fresh0_copy((me + k) % PLANE, crossing).wait_send()

    @pl.when(relays_fresh0)
    def _():
        fresh0_z.wait_send()

    for copy in meta_copies:
        copy.wait_send()
    zrow_copy.wait_send()

    for i in range(6, 8):
        z_copy(i).wait_send()

    for group in range(4):
        sum_copy(group).wait_send()
    for sweep, (x_ref, k_ref) in enumerate(((x0, k0), (x1, k1))):
        wait_halo_sent(sweep, x_ref, k_ref)

    @pl.loop(0, FRAMES)
    def _(frame):
        wait_bytes(ys.at[slot(frame)], s_back.at[frame])

    @pl.when(q % 4 == 0)
    def _():
        for i in range(RELAYED):
            onward_copy(i).wait_send()


def local(state, fresh, frame_level, request, q_table, k_table, step_size, reference_kv):
    block = FRAMES * FT
    dma = pltpu.SemaphoreType.DMA
    vmem = pl.BlockSpec(memory_space=pltpu.VMEM)
    return pl.pallas_call(
        kernel,
        out_shape=jax.ShapeDtypeStruct(state.shape, state.dtype),
        in_specs=[pl.BlockSpec(memory_space=pltpu.HBM)] * 8,
        out_specs=vmem,
        scratch_shapes=[
            pltpu.VMEM((HALF, HD), BF16),
            pltpu.VMEM((block // 2, WIDTH), BF16),
            pltpu.VMEM((FT, WIDTH), BF16),
            pltpu.VMEM((FT, WIDTH), BF16),
            pltpu.VMEM((block + 2 * FT, WIDTH), BF16),
            pltpu.VMEM((block + 2 * FT, WIDTH), BF16),
            pltpu.VMEM((block + 2 * FT, WIDTH), BF16),
            pltpu.VMEM((block + 2 * FT, WIDTH), BF16),
            pltpu.VMEM((block, WIDTH), BF16),
            pltpu.VMEM((block, WIDTH), BF16),
            pltpu.VMEM((2, block // 2, WIDTH), BF16),
            pltpu.VMEM((PLANE, 8, 128), F32),
            pltpu.VMEM((2, PLANE, 128), F32),
            pltpu.VMEM((block, 128), F32),
            pltpu.VMEM((4, 8, 128), F32),
            pltpu.VMEM((4, 8, 128), F32),
            pltpu.VMEM((4, 8, 128), F32),
            pltpu.VMEM((4, PLANE, 8, 128), F32),
            pltpu.VMEM(frame_level.shape, jnp.int32),
            pltpu.VMEM(frame_level.shape, jnp.int32),
            pltpu.VMEM(request.shape, jnp.int32),
            pltpu.VMEM(request.shape, jnp.int32),
            pltpu.VMEM((2, 128, WIDTH), F32),
            pltpu.VMEM((1, step_size.shape[0]), F32),
            pltpu.VMEM(reference_kv.shape, BF16),
            pltpu.VMEM((128, 128), F32),
            pltpu.VMEM((2, FRAMES, WIDTH), F32),
            pltpu.VMEM((2, FRAMES, WIDTH), F32),
            pltpu.VMEM((2, FRAMES, WIDTH), F32),
            pltpu.VMEM((2, FT, WIDTH), BF16),
            pltpu.VMEM((2, FT, WIDTH), BF16),
            dma((PLANE,)), dma((PLANE,)), dma((PLANE,)), dma((PLANE,)), dma((PLANE,)), dma((PLANE,)),
            dma((8,)), dma((8,)), dma, dma,
            dma((2, 4)), dma((2, 4)), dma((2,)), dma((2,)), dma((4,)), dma((4,)), dma((4, PLANE)), dma((4, PLANE)),
            dma((FRAMES,)), dma((2, 8)), dma((2, PLANE)), dma((2, PLANE)),
            dma((PLANE,)), dma((2,)), dma((PLANE,)), dma((2,)), dma, dma,
            dma((7,)), pltpu.VMEM((RELAYED * FT, WIDTH), BF16), dma((RELAYED,)), dma((RELAYED,)),
        ],
        compiler_params=pltpu.CompilerParams(
            collective_id=0, has_side_effects=True, vmem_limit_bytes=60 << 20
        ),
    )(state, fresh[0], frame_level, request, q_table, k_table, step_size[None, :], reference_kv)


def solution(mesh):
    placed = (
        P(("queue", "heads"), None),
        P(None, "heads", None),
        P(None, "queue"),
        P(None, "queue"),
        P(None, "heads"),
        P(None, "heads"),
        P(),
        P(None, None, None, "heads"),
    )
    return jax.shard_map(
        local, mesh=mesh, in_specs=placed, out_specs=P(("queue", "heads"), None), check_vma=False
    )
```

```python
import functools
import math

import jax
import jax.numpy as jnp
from jax import lax
from jax.experimental import pallas as pl
from jax.experimental.pallas import tpu as pltpu
from jax.sharding import PartitionSpec as P

FT = 256
FRAMES = 16
HALF = 128
HD = 4096
WIDTH = 128
QUEUE = 16
PLANE = 16
ROWS = 256
RELAYED = 6

epsilon = 1e-06
far_below = -1e30
MESH = pl.DeviceIdType.MESH
HIGHEST = lax.Precision.HIGHEST
BF16 = jnp.bfloat16
F32 = jnp.float32


def dot_nt(a, b, precision=None):
    return lax.dot_general(
        a, b, (((1,), (1,)), ((), ())), precision=precision, preferred_element_type=F32
    )


def slot(index):
    return pl.ds(pl.multiple_of(index * FT, FT), FT)


def half_rows(index):
    return pl.ds(pl.multiple_of(index * HALF, HALF), HALF)


def columns(head):
    return pl.ds(pl.multiple_of(head * WIDTH, WIDTH), WIDTH)


def kernel(
    state, fresh, frame_level, request, q_tab, k_tab, step_size, ref_in,
    out,
    src, cross, fresh0, fresh0_cross,
    x0, k0, x1, k1, qs, ys, back,
    r_in, r_rows, r_full, sums, sums_other, sums_both, sums_all,
    levels, levels_next, wanted, wanted_next, tables, step_tab, ref_kv, level_pad,
    q_scale, k_scale, step_rows, ref_k, ref_v,
    s_cross, r_cross, s_stay, r_stay, s_row, r_row, s_z, r_z, s_zrow, r_zrow,
    s_halo, r_halo, s_meta, r_meta, s_sum, r_sum, s_all, r_all,
    s_back, r_back, s_out, r_out, s_f, r_f, s_fc, r_fc, s_fz, r_fz,
    load, via, s_via, r_via,
):
    q = lax.axis_index("queue")
    h = lax.axis_index("heads")
    z_hi = (h // 4) % 2
    me = (h // 8) * 4 + h % 4
    other = h + 4 - 8 * z_hi
    q_next = (q + 1) % QUEUE
    q_prev = (q + QUEUE - 1) % QUEUE
    last = q == QUEUE - 1

    def head_of(place, part):
        return (place // 4) * 8 + part * 4 + place % 4

    def remote(a, b, send, recv, to_q, to_h):
        return pltpu.make_async_remote_copy(
            src_ref=a, dst_ref=b, send_sem=send, recv_sem=recv,
            device_id=(to_q, to_h), device_id_type=MESH,
        )

    def own_frame(i):
        flip = ((i // 2) + z_hi) % 2
        return i + flip * (15 - 2 * i)

    def compact(frame):
        return (frame // 4) * 2 + frame % 2

    barrier = pltpu.get_barrier_semaphore()

    def greet(to_q, to_h):
        pl.semaphore_signal(barrier, inc=1, device_id=(to_q, to_h), device_id_type=MESH)

    greet(q, other)
    greet(q_next, other)
    greet(q_prev, other)
    greet(q_next, h)
    greet(q_prev, h)

    relays_fresh0 = jnp.logical_and(q == 1, z_hi == 0)
    takes_fresh0 = jnp.logical_and(last, z_hi == 1)

    @pl.when(relays_fresh0)
    def _():
        greet(QUEUE - 1, other)

    @pl.when(takes_fresh0)
    def _():
        greet(1, other)


    @pl.loop(1, PLANE)
    def _(k):
        greet(q, head_of((me + k) % PLANE, z_hi))

    holds_first = jnp.logical_and(h // 8 == 0, jnp.logical_and(z_hi == 0, h % 4 < 2))
    use_fresh = jnp.logical_and(last, jnp.logical_not(holds_first))

    @pl.when(use_fresh)
    def _():
        pltpu.make_async_copy(fresh, src, load.at[0]).start()

    @pl.when(jnp.logical_not(use_fresh))
    def _():
        pltpu.make_async_copy(state, src, load.at[0]).start()

    tables[...] = jnp.zeros_like(tables)
    loads = [
        pltpu.make_async_copy(a, b, load.at[1 + index])
        for index, (a, b) in enumerate((
            (frame_level, levels), (request, wanted), (step_size, step_tab),
            (q_tab, tables.at[0, 0:48]), (k_tab, tables.at[1, 0:48]), (ref_in, ref_kv),
        ))
    ]
    for copy in loads:
        copy.start()
    pltpu.make_async_copy(state, src, load.at[0]).wait()

    total = jnp.zeros((HALF, WIDTH), F32)
    for block in range(HD // WIDTH):
        part = src[:, block * WIDTH : (block + 1) * WIDTH].astype(F32)
        total = total + part * part
    ones = jnp.ones((8, WIDTH), F32)
    own_row = lax.rsqrt(dot_nt(ones, total, HIGHEST) / HD + epsilon)

    def modulation(sweep, level_ref, wanted_ref):
        level_pad[...] = jnp.zeros_like(level_pad)
        level_pad[0:2, 0:FRAMES] = level_ref[...].astype(F32)
        turned = jnp.transpose(level_pad[...])
        own = turned[0:FRAMES, sweep : sweep + 1]
        lanes = lax.broadcasted_iota(jnp.int32, (FRAMES, 128), 1).astype(F32)
        one_hot = (jnp.broadcast_to(own, (FRAMES, 128)) == lanes).astype(F32)
        for table, result in ((0, q_scale), (1, k_scale)):
            result[sweep] = lax.dot_general(
                one_hot, tables[table], (((1,), (0,)), ((), ())),
                precision=HIGHEST, preferred_element_type=F32,
            )
        picked = jnp.sum(one_hot[:, 0:48] * step_tab[...], axis=1, keepdims=True)
        step_rows[sweep] = jnp.broadcast_to(picked, (FRAMES, WIDTH))
        choice = jnp.broadcast_to(wanted_ref[sweep : sweep + 1, :], (FT, WIDTH))
        for part, result in ((0, ref_k), (1, ref_v)):
            chosen = jnp.zeros((FT, WIDTH), F32)
            for index in range(ref_kv.shape[1]):
                chosen = jnp.where(choice == index, ref_kv[part, index].astype(F32), chosen)
            result[sweep] = chosen.astype(BF16)

    for copy in loads:
        copy.wait()
    modulation(0, levels, wanted)

    r_in[me] = own_row
    extra = jnp.logical_or(relays_fresh0, takes_fresh0).astype(jnp.int32)
    pl.semaphore_wait(barrier, PLANE - 1 + 5 + extra)

    def row_copy(place):
        return remote(r_in.at[me], r_in.at[me], s_row.at[place], r_row.at[me], q, head_of(place, z_hi))

    def cross_copy(place):
        return remote(
            src.at[:, columns(head_of(place, 1 - z_hi))], cross.at[half_rows(me)],
            s_cross.at[place], r_cross.at[me], q, head_of(place, z_hi),
        )

    def stay_rows(place):
        return half_rows(2 + (place // 4) * 8 + z_hi * 4 + place % 4)

    def stay_copy(place):
        return remote(
            src.at[:, columns(head_of(place, z_hi))], x0.at[stay_rows(me)],
            s_stay.at[place], r_stay.at[me], q, head_of(place, z_hi),
        )

    @pl.loop(1, PLANE)
    def _(k):
        row_copy((me + k) % PLANE).start()

    own_cross = pltpu.make_async_copy(
        src.at[:, columns(other)], cross.at[half_rows(me)], r_cross.at[me]
    )
    own_cross.start()

    @pl.loop(1, PLANE)
    def _(k):
        cross_copy((me + k) % PLANE).start()

    own_stay = pltpu.make_async_copy(src.at[:, columns(h)], x0.at[stay_rows(me)], r_stay.at[me])
    own_stay.start()

    @pl.loop(1, PLANE)
    def _(k):
        stay_copy((me + k) % PLANE).start()

    meta_copies = [
        remote(levels, levels_next, s_meta.at[0], r_meta.at[0], q_prev, h),
        remote(wanted, wanted_next, s_meta.at[1], r_meta.at[1], q_prev, h),
    ]
    for copy in meta_copies:
        copy.start()

    def fresh0_copy(place, crossing):
        half = h % 4
        part = z_hi + crossing * (1 - 2 * z_hi)
        target = fresh0_cross if crossing else fresh0
        send, recv = (s_fc, r_fc) if crossing else (s_f, r_f)
        return remote(
            fresh.at[:, columns(head_of(place, part))], target.at[half_rows(half)],
            send.at[place], recv.at[half], q, head_of(place, z_hi),
        )

    gives_fresh0 = jnp.logical_and(last, holds_first)
    gives_cross0 = jnp.logical_and(q == 1, holds_first)

    for gives, crossing, head, target, recv in (
        (gives_cross0, 1, other, fresh0_cross, r_fc), (gives_fresh0, 0, h, fresh0, r_f),
    ):
        @pl.when(gives)
        def _():
            half = h % 4
            pltpu.make_async_copy(
                fresh.at[:, columns(head)], target.at[half_rows(half)], recv.at[half]
            ).start()

            @pl.loop(1, PLANE)
            def _(k):
                fresh0_copy((me + k) % PLANE, crossing).start()

    def wait_bytes(ref, sem):
        pltpu.make_async_copy(ref, ref, sem).wait()

    @pl.loop(1, PLANE)
    def _(k):
        place = (me + k) % PLANE
        wait_bytes(r_in.at[place], r_row.at[place])

    for place in range(PLANE):
        r_rows[z_hi, place : place + 1, :] = r_in[place, 0:1, :]
    zrow_copy = remote(r_rows.at[z_hi], r_rows.at[z_hi], s_zrow, r_zrow, q, other)
    zrow_copy.start()

    def z_copy(i):
        frame = own_frame(i)
        return remote(
            cross.at[slot(compact(frame))], x0.at[slot(frame + 1)], s_z.at[i], r_z.at[i], q, other
        )

    def send_z(i):
        c = compact(own_frame(i))
        wait_bytes(cross.at[half_rows(2 * c)], r_cross.at[2 * c])
        wait_bytes(cross.at[half_rows(2 * c + 1)], r_cross.at[2 * c + 1])
        z_copy(i).start()

    fresh0_z = remote(fresh0_cross, fresh0, s_fz, r_fz, QUEUE - 1, other)

    def send_fresh0():
        @pl.when(relays_fresh0)
        def _():
            for half in range(2):
                wait_bytes(fresh0_cross.at[half_rows(half)], r_fc.at[half])
            fresh0_z.start()

    send_z(0)
    send_z(1)
    send_fresh0()

    def spread(rows_value, count, target_rows):
        padded = jnp.concatenate(
            [rows_value, jnp.zeros((128 - rows_value.shape[0], 128), F32)], axis=0
        )
        turned = jnp.transpose(padded)
        for index in range(count):
            r_full[target_rows(index), :] = jnp.broadcast_to(turned[:, index : index + 1], (128, 128))

    wait_bytes(r_rows.at[1 - z_hi], r_zrow)

    def first_rows(index):
        part, place = index // PLANE, index % PLANE
        chunk = (place // 4) * 8 + part * 4 + place % 4
        return half_rows(chunk)

    spread(jnp.concatenate([r_rows[0], r_rows[1]], axis=0), 2 * PLANE, first_rows)

    def prepare(sweep, x_ref, k_ref, frame):
        normed = x_ref[slot(frame + 1), :].astype(F32) * r_full[slot(frame), :]
        qs[slot(frame), :] = (normed * q_scale[sweep, pl.ds(frame, 1), :]).astype(BF16)
        k_ref[slot(frame + 1), :] = (normed * k_scale[sweep, pl.ds(frame, 1), :]).astype(BF16)

    factor = math.log2(math.e) / math.sqrt(WIDTH)

    def attend(sweep, x_ref, k_ref, frame, no_prev, no_next, target, target_slot):
        before = jnp.where(jnp.logical_and(frame == 0, no_prev), far_below, 0.0).astype(F32)
        after = jnp.where(jnp.logical_and(frame == FRAMES - 1, no_next), far_below, 0.0).astype(F32)
        step = step_rows[sweep, pl.ds(frame, 1), :]

        @pl.loop(0, FT // ROWS)
        def _(chunk):
            start = pl.multiple_of(frame * FT + chunk * ROWS, ROWS)
            query = qs[pl.ds(start, ROWS), :]
            scores = []
            for part in range(3):
                scores.append(dot_nt(query, k_ref[slot(frame + part), :]))
            scores[0] = scores[0] + before
            scores[2] = scores[2] + after
            scores.append(dot_nt(query, ref_k[sweep]))
            high = jnp.maximum(
                jnp.maximum(scores[0], scores[1]), jnp.maximum(scores[2], scores[3])
            )
            high = jnp.max(high, axis=1, keepdims=True)
            probs = [jnp.exp2((part - high) * factor) for part in scores]
            weight = (probs[0] + probs[1]) + (probs[2] + probs[3])
            weight = jnp.sum(weight, axis=1, keepdims=True)
            result = jnp.dot(probs[3].astype(BF16), ref_v[sweep], preferred_element_type=F32)
            for part in range(3):
                result = result + jnp.dot(
                    probs[part].astype(BF16), x_ref[slot(frame + part), :],
                    preferred_element_type=F32,
                )
            attn = (result / weight).astype(BF16).astype(F32)
            held = x_ref[pl.ds(start + FT, ROWS), :].astype(F32)
            place = pl.multiple_of(target_slot * FT + chunk * ROWS, ROWS)
            target[pl.ds(place, ROWS), :] = (held + step * attn).astype(BF16)

    def halo_copies(sweep, x_ref, k_ref):
        copies = []
        for index, (ref, here, there, to_q) in enumerate((
            (k_ref, 1, 17, q_prev), (x_ref, 1, 17, q_prev),
            (k_ref, 16, 0, q_next), (x_ref, 16, 0, q_next),
        )):
            copies.append(remote(
                ref.at[slot(here)], ref.at[slot(there)],
                s_halo.at[sweep, index], r_halo.at[sweep, index], to_q, h,
            ))
        return copies

    def halo_roles(sweep):
        if sweep == 0:
            return q != 0, q < QUEUE - 2, q != QUEUE - 1, jnp.logical_and(q != 0, q != QUEUE - 1)
        return q != QUEUE - 1, q != QUEUE - 2, q != QUEUE - 2, q != QUEUE - 1

    def start_halo(sweep, x_ref, k_ref):
        copies = halo_copies(sweep, x_ref, k_ref)
        to_prev, to_next, from_next, from_prev = halo_roles(sweep)
        for group, wanted_here in ((copies[:2], to_prev), (copies[2:], to_next)):
            @pl.when(wanted_here)
            def _():
                for copy in group:
                    copy.start()
        for rim, absent in ((17, jnp.logical_not(from_next)), (0, jnp.logical_not(from_prev))):
            @pl.when(absent)
            def _():
                for ref in (x_ref, k_ref):
                    ref[slot(rim), :] = jnp.zeros((FT, WIDTH), BF16)

    def wait_halo(sweep, x_ref, k_ref):
        copies = halo_copies(sweep, x_ref, k_ref)
        _, _, from_next, from_prev = halo_roles(sweep)
        for group, wanted_here in ((copies[:2], from_next), (copies[2:], from_prev)):
            @pl.when(wanted_here)
            def _():
                for copy in group:
                    copy.wait_recv()

    def wait_halo_sent(sweep, x_ref, k_ref):
        copies = halo_copies(sweep, x_ref, k_ref)
        to_prev, to_next, _, _ = halo_roles(sweep)
        for group, wanted_here in ((copies[:2], to_prev), (copies[2:], to_next)):
            @pl.when(wanted_here)
            def _():
                for copy in group:
                    copy.wait_send()

    def arrive(i):
        frame = own_frame(i)
        c = compact(frame)
        for half in range(2):
            wait_bytes(x0.at[half_rows(2 * (frame + 1) + half)], r_stay.at[2 * c + half])
        wait_bytes(x0.at[slot(16 - frame)], r_z.at[i])

    def first_pairs(i0, count):
        @pl.loop(0, 2 * count)
        def _(k):
            i = i0 + k // 2
            frame = i + (k % 2) * (15 - 2 * i)

            @pl.when(jnp.logical_not(last))
            def _():
                attend(0, x0, k0, frame, q == 0, last, x1, frame + 1)

            @pl.when(last)
            def _():
                x1[slot(frame + 1), :] = x0[slot(frame + 1), :]

    def take_fresh0():
        @pl.when(jnp.logical_and(last, z_hi == 0))
        def _():
            for half in range(2):
                wait_bytes(fresh0.at[half_rows(half)], r_f.at[half])

        @pl.when(takes_fresh0)
        def _():
            wait_bytes(fresh0, r_fz)

        @pl.when(last)
        def _():
            x1[slot(1), :] = fresh0[...]

    def sum_copy(group):
        return remote(
            sums.at[group], sums_other.at[group], s_sum.at[group], r_sum.at[group], q, other
        )

    def start_sums(group):
        for index in range(4):
            i = 2 * group + index // 2
            frame = i if index % 2 == 0 else 15 - i
            held = x1[slot(frame + 1), :].astype(F32)
            row = dot_nt(ones, held * held, HIGHEST)
            sums[group, 2 * index : 2 * index + 1, :] = row[0:1, 0:128]
            sums[group, 2 * index + 1 : 2 * index + 2, :] = row[0:1, 128:256]
        sum_copy(group).start()

    def all_copy(group, place):
        return remote(
            sums_both.at[group], sums_all.at[group, me],
            s_all.at[group, place], r_all.at[group, me], q, head_of(place, z_hi),
        )

    def spread_sums(group):
        wait_bytes(sums_other.at[group], r_sum.at[group])
        both = sums[group] + sums_other[group]
        sums_both[group] = both

        @pl.loop(1, PLANE)
        def _(k):
            all_copy(group, (me + k) % PLANE).start()

        sums_all[group, me] = both

    def prepare_group(group):
        @pl.loop(1, PLANE)
        def _(k):
            place = (me + k) % PLANE
            wait_bytes(sums_all.at[group, place], r_all.at[group, place])

        whole = sums_all[group, 0]
        for place in range(1, PLANE):
            whole = whole + sums_all[group, place]
        rows = lax.rsqrt(whole / HD + epsilon)

        def group_rows(index):
            i = 2 * group + index // 4
            frame = i if (index // 2) % 2 == 0 else 15 - i
            return half_rows(2 * frame + index % 2)

        spread(rows, 8, group_rows)

        @pl.loop(0, 4)
        def _(k):
            i = 2 * group + k // 2
            prepare(1, x1, k1, i + (k % 2) * (15 - 2 * i))

    def back_copy(frame):
        moves = ((frame // 2) + z_hi) % 2
        return remote(
            ys.at[slot(frame)], back.at[moves, slot(compact(frame))],
            s_back.at[frame], r_back.at[moves, compact(frame)],
            q_next, h + moves * (4 - 8 * z_hi),
        )

    def is_relayed(i, frame):
        moves = ((frame // 2) + z_hi) % 2
        far = jnp.where(last, 0, 1)
        return jnp.logical_and(q % 4 == 3, jnp.logical_and(moves == far, i < RELAYED))

    def via_copy(i, frame):
        near = h + jnp.where(last, 1, 0) * (4 - 8 * z_hi)
        return remote(
            ys.at[slot(frame)], via.at[slot(i)], s_back.at[frame], r_via.at[i], q_next, near
        )

    def onward_copy(i):
        c = compact(15 - own_frame(i))
        part = jnp.where(q == 0, 0, 1)
        return remote(
            via.at[slot(i)], back.at[part, slot(c)], s_via.at[i], r_back.at[part, c], q, other
        )

    def relay_back(i):
        @pl.when(q % 4 == 0)
        def _():
            wait_bytes(via.at[slot(i)], r_via.at[i])
            onward_copy(i).start()

    def second_pairs(i0, count):
        @pl.loop(0, 2 * count)
        def _(k):
            i = i0 + k // 2
            frame = i + (k % 2) * (15 - 2 * i)
            attend(1, x1, k1, frame, last, q == QUEUE - 2, ys, frame)

            @pl.when(is_relayed(i, frame))
            def _():
                via_copy(i, frame).start()

            @pl.when(jnp.logical_not(is_relayed(i, frame)))
            def _():
                back_copy(frame).start()

    def prepare_pair(i):
        @pl.loop(0, 2)
        def _(k):
            prepare(0, x0, k0, i + k * (15 - 2 * i))

    def next_z(i):
        z_copy(i - 2).wait_send()
        send_z(i)

    next_z(2)
    arrive(0)
    prepare_pair(0)
    start_halo(0, x0, k0)
    next_z(3)
    arrive(1)
    prepare_pair(1)
    wait_halo(0, x0, k0)
    first_pairs(0, 1)
    next_z(4)
    arrive(2)
    prepare_pair(2)
    first_pairs(1, 1)
    next_z(5)
    arrive(3)
    prepare_pair(3)
    first_pairs(2, 1)
    for index in range(2):
        meta_copies[index].wait_recv()
    modulation(1, levels_next, wanted_next)
    next_z(6)
    take_fresh0()
    start_sums(0)
    arrive(4)
    prepare_pair(4)
    first_pairs(3, 1)
    start_sums(1)
    next_z(7)
    spread_sums(0)
    arrive(5)
    prepare_pair(5)
    first_pairs(4, 1)
    spread_sums(1)
    prepare_group(0)
    start_halo(1, x1, k1)
    arrive(6)
    prepare_pair(6)
    first_pairs(5, 1)
    start_sums(2)
    arrive(7)
    prepare_pair(7)
    first_pairs(6, 2)
    start_sums(3)
    spread_sums(2)
    spread_sums(3)
    wait_halo(1, x1, k1)
    second_pairs(0, 1)
    prepare_group(1)
    second_pairs(1, 2)
    relay_back(0)
    prepare_group(2)
    second_pairs(3, 2)
    relay_back(1)
    relay_back(2)
    prepare_group(3)
    second_pairs(5, 3)
    relay_back(3)
    relay_back(4)
    relay_back(5)

    def out_copy(part, c, half):
        place = 2 * c + half
        head = h + part * (4 - 8 * z_hi)
        return remote(
            back.at[part, half_rows(place)], out.at[:, columns(head)],
            s_out.at[part, place], r_out.at[part, me], q, head_of(place, z_hi),
        )

    def out_local(part):
        head = h + part * (4 - 8 * z_hi)
        return pltpu.make_async_copy(
            back.at[part, half_rows(me)], out.at[:, columns(head)], r_out.at[part, me]
        )

    @pl.loop(0, 16)
    def _(k):
        c = compact(own_frame(k // 2))
        part = k % 2
        wait_bytes(back.at[part, slot(c)], r_back.at[part, c])
        for half in range(2):
            place = 2 * c + half

            @pl.when(place == me)
            def _():
                out_local(part).start()

            @pl.when(place != me)
            def _():
                out_copy(part, c, half).start()

    @pl.loop(0, 2 * PLANE)
    def _(k):
        part, place = k // PLANE, k % PLANE
        head = head_of(place, z_hi + part - 2 * z_hi * part)
        wait_bytes(out.at[:, columns(head)], r_out.at[part, place])

    @pl.loop(1, PLANE)
    def _(k):
        place = (me + k) % PLANE
        row_copy(place).wait_send()
        cross_copy(place).wait_send()
        stay_copy(place).wait_send()
        for part in range(2):
            out_copy(part, place // 2, place % 2).wait_send()
        for group in range(4):
            all_copy(group, place).wait_send()

    for gives, crossing in ((gives_cross0, 1), (gives_fresh0, 0)):
        @pl.when(gives)
        def _():
            @pl.loop(1, PLANE)
            def _(k):
                fresh0_copy((me + k) % PLANE, crossing).wait_send()

    @pl.when(relays_fresh0)
    def _():
        fresh0_z.wait_send()

    for copy in meta_copies:
        copy.wait_send()
    zrow_copy.wait_send()

    for i in range(6, 8):
        z_copy(i).wait_send()

    for group in range(4):
        sum_copy(group).wait_send()
    for sweep, (x_ref, k_ref) in enumerate(((x0, k0), (x1, k1))):
        wait_halo_sent(sweep, x_ref, k_ref)

    @pl.loop(0, FRAMES)
    def _(frame):
        wait_bytes(ys.at[slot(frame)], s_back.at[frame])

    @pl.when(q % 4 == 0)
    def _():
        for i in range(RELAYED):
            onward_copy(i).wait_send()


def local(state, fresh, frame_level, request, q_table, k_table, step_size, reference_kv):
    block = FRAMES * FT
    dma = pltpu.SemaphoreType.DMA
    vmem = pl.BlockSpec(memory_space=pltpu.VMEM)
    return pl.pallas_call(
        kernel,
        out_shape=jax.ShapeDtypeStruct(state.shape, state.dtype),
        in_specs=[pl.BlockSpec(memory_space=pltpu.HBM)] * 8,
        out_specs=vmem,
        scratch_shapes=[
            pltpu.VMEM((HALF, HD), BF16),
            pltpu.VMEM((block // 2, WIDTH), BF16),
            pltpu.VMEM((FT, WIDTH), BF16),
            pltpu.VMEM((FT, WIDTH), BF16),
            pltpu.VMEM((block + 2 * FT, WIDTH), BF16),
            pltpu.VMEM((block + 2 * FT, WIDTH), BF16),
            pltpu.VMEM((block + 2 * FT, WIDTH), BF16),
            pltpu.VMEM((block + 2 * FT, WIDTH), BF16),
            pltpu.VMEM((block, WIDTH), BF16),
            pltpu.VMEM((block, WIDTH), BF16),
            pltpu.VMEM((2, block // 2, WIDTH), BF16),
            pltpu.VMEM((PLANE, 8, 128), F32),
            pltpu.VMEM((2, PLANE, 128), F32),
            pltpu.VMEM((block, 128), F32),
            pltpu.VMEM((4, 8, 128), F32),
            pltpu.VMEM((4, 8, 128), F32),
            pltpu.VMEM((4, 8, 128), F32),
            pltpu.VMEM((4, PLANE, 8, 128), F32),
            pltpu.VMEM(frame_level.shape, jnp.int32),
            pltpu.VMEM(frame_level.shape, jnp.int32),
            pltpu.VMEM(request.shape, jnp.int32),
            pltpu.VMEM(request.shape, jnp.int32),
            pltpu.VMEM((2, 128, WIDTH), F32),
            pltpu.VMEM((1, step_size.shape[0]), F32),
            pltpu.VMEM(reference_kv.shape, BF16),
            pltpu.VMEM((128, 128), F32),
            pltpu.VMEM((2, FRAMES, WIDTH), F32),
            pltpu.VMEM((2, FRAMES, WIDTH), F32),
            pltpu.VMEM((2, FRAMES, WIDTH), F32),
            pltpu.VMEM((2, FT, WIDTH), BF16),
            pltpu.VMEM((2, FT, WIDTH), BF16),
            dma((PLANE,)), dma((PLANE,)), dma((PLANE,)), dma((PLANE,)), dma((PLANE,)), dma((PLANE,)),
            dma((8,)), dma((8,)), dma, dma,
            dma((2, 4)), dma((2, 4)), dma((2,)), dma((2,)), dma((4,)), dma((4,)), dma((4, PLANE)), dma((4, PLANE)),
            dma((FRAMES,)), dma((2, 8)), dma((2, PLANE)), dma((2, PLANE)),
            dma((PLANE,)), dma((2,)), dma((PLANE,)), dma((2,)), dma, dma,
            dma((7,)), pltpu.VMEM((RELAYED * FT, WIDTH), BF16), dma((RELAYED,)), dma((RELAYED,)),
        ],
        compiler_params=pltpu.CompilerParams(
            collective_id=0, has_side_effects=True, vmem_limit_bytes=60 << 20
        ),
    )(state, fresh[0], frame_level, request, q_table, k_table, step_size[None, :], reference_kv)


def solution(mesh):
    placed = (
        P(("queue", "heads"), None),
        P(None, "heads", None),
        P(None, "queue"),
        P(None, "queue"),
        P(None, "heads"),
        P(None, "heads"),
        P(),
        P(None, None, None, "heads"),
    )
    return jax.shard_map(
        local, mesh=mesh, in_specs=placed, out_specs=P(("queue", "heads"), None), check_vma=False
    )
```
